512 devices in a mesh: dp: 32 (over y, x_hi, core), tensor: 16 (over z, x_lo).
Axes of the slice: x: 4 (x_hi: 2, x_lo: 2; x = x_hi * 2 + x_lo), y: 8, z: 8, core: 2. Of those that a mesh axis runs over, the one named last changes fastest.
Arguments:
- tokens: bfloat16 [65536, 896], P(('dp', 'tensor')), parts along dimension 0, may hold values from -6 to 6
- smooth_scale: float32 [896], replicated, may hold values from 0.25 to 4
- gate_weight: bfloat16 [4864, 896], P('tensor'), may hold values from -0.1875 to 0.1875
- up_weight: bfloat16 [4864, 896], P('tensor'), may hold values from -0.1875 to 0.1875
- down_weight: bfloat16 [4864, 896], P('tensor'), may hold values from -0.078125 to 0.078125
Outputs:
- mixed: bfloat16 [65536, 896], P(('dp', 'tensor')), parts along dimension 0
The draws below stay inside these ranges and needn't reach their ends.
There are 32 independent parts, one for each index of `dp`. The reference program is written for one: setup_inputs(seed, part) draws one part's arguments, and reference() takes and returns one part's arrays. A program takes and returns all parts, laid end to end along the dimension named above; an argument that names none is the same for every part. Nothing has to cross between parts.
All inputs are finite; a program needn't handle non-finite values.
Results may differ from the reference program's by a relative error of at most 0.0064.
Values may be sent and summed in bfloat16 or wider, within the bound.
A program may use at most 64 MiB of HBM per device.

```python
import math
import jax
import jax.numpy as jnp

D = 896
FF = 4864
TOKENS = 2048


def shard_levels(rng, dims, pieces, low, largest):
    factor_of, own = 1.0, jax.random.fold_in(rng, 6)
    for dim, parts in pieces:
        draws = jnp.exp(jax.random.uniform(jax.random.fold_in(own, dim), (parts,), jnp.float32, low / len(pieces), largest / len(pieces)))
        factor_of = factor_of * jnp.repeat(draws, dims[dim] // parts).reshape([-1 if axis == dim else 1 for axis in range(len(dims))])
    return factor_of


def gaussian(key, extent, spread, most, split=(), dtype=jnp.bfloat16):
    array = spread * jax.random.normal(key, extent, jnp.float32)
    if split:
        array = array * shard_levels(key, extent, split, -0.22, 0.18)
    return jnp.clip(array, -most, most).astype(dtype)


def setup_inputs(seed: int = 0, part: int = 0) -> dict:
    seeds = jax.random.split(jax.random.key(seed), 6)
    own_keys = jax.random.split(jax.random.fold_in(seeds[5], part), 6)
    return {
        "tokens": gaussian(own_keys[0], (TOKENS, D), 1.0, 6.0, ((0, 16),)),
        "smooth_scale": jnp.clip(jnp.exp(jax.random.uniform(seeds[1], (D,), jnp.float32, math.log(0.25), math.log(4.0))), 0.25, 4.0),
        "gate_weight": gaussian(seeds[2], (FF, D), D ** -0.5, 0.1875, ((0, 16),)),
        "up_weight": gaussian(seeds[3], (FF, D), D ** -0.5, 0.1875, ((0, 16),)),
        "down_weight": gaussian(seeds[4], (FF, D), FF ** -0.5, 0.078125, ((0, 16),)),
    }


def reference(tokens, smooth_scale, gate_weight, up_weight, down_weight):
    smoothed = (tokens.astype(jnp.float32) / smooth_scale[None, :]).astype(jnp.bfloat16)
    gate_out = jnp.dot(smoothed, gate_weight.T, preferred_element_type=jnp.float32)
    up_out = jnp.dot(smoothed, up_weight.T, preferred_element_type=jnp.float32)
    hidden = (jax.nn.silu(gate_out) * up_out).astype(jnp.bfloat16)
    mixed = jnp.dot(hidden, down_weight, preferred_element_type=jnp.float32)
    return mixed.astype(jnp.bfloat16)
```

```python
import jax
import jax.numpy as jnp
from jax import lax
from jax.experimental import pallas as pl
from jax.experimental.pallas import tpu as pltpu
from jax.sharding import PartitionSpec as P

MESH = pl.DeviceIdType.MESH
BF16, F32 = jnp.bfloat16, jnp.float32
ROWS_BY_COLS = (((1,), (1,)), ((), ()))
UP, DOWN = 0, 1
PIECES = 4


def kernel(
    tokens_ref, scale_ref, gate_ref, up_ref, down_ref, out_ref,
    raw, x, w, acc, sums, came,
    load_sem, ag_send, ag_recv, rs_send, rs_recv, w_send, w_recv, f_send, f_recv,
):
    dp, t = lax.axis_index("dp"), lax.axis_index("tensor")
    core, x_hi = lax.rem(dp, 2), lax.rem(dp // 2, 2)
    other_t = t + 1 - 2 * lax.rem(t, 2)
    towards = ((dp, lax.rem(t + 2, 16)), (dp, lax.rem(t + 14, 16)))
    sibling = (dp + 1 - 2 * core, t)
    partner = (dp + core * (2 - 4 * x_hi), other_t)

    rows = tokens_ref.shape[0]
    part = rows // PIECES
    half = rows // 2
    units = gate_ref.shape[0]
    big = (units // 2 + 15) // 16 * 16
    small = units - big

    loads = [pltpu.make_async_copy(tokens_ref, raw, load_sem.at[0])]
    for i, ref in enumerate((gate_ref, up_ref, down_ref)):
        loads.append(pltpu.make_async_copy(ref, w.at[i, pl.ds(0, units)], load_sem.at[i + 1]))
    for load in loads:
        load.start()

    barrier = pltpu.get_barrier_semaphore()
    for device in (*towards, sibling, partner):
        pl.semaphore_signal(barrier, inc=1, device_id=device, device_id_type=MESH)

    loads[0].wait()
    x[0] = (raw[...].astype(F32) / scale_ref[...]).astype(BF16)
    pl.semaphore_wait(barrier, 4)

    def gather(way, hop, piece):
        here = hop if way == UP else (8 - hop) % 8
        there = hop + 1 if way == UP else 7 - hop
        at = pl.ds(piece * part, part)
        return pltpu.make_async_remote_copy(
            src_ref=x.at[here, at],
            dst_ref=x.at[there, at],
            send_sem=ag_send.at[way, hop, piece],
            recv_sem=ag_recv.at[way, hop, piece],
            device_id=towards[way],
            device_id_type=MESH,
        )

    first = ((2, 3), (0, 1))
    second = ((0, 1), (2, 3))

    def pass_on(hop, piece_of):
        for way in (UP, DOWN):
            if hop:
                gather(way, hop - 1, piece_of(way)).wait_recv()
            gather(way, hop, piece_of(way)).start()

    def from_partner(i):
        which, start, size = ((core, 0, big), (core, big, small), (2, core * small, big))[i]
        return pltpu.make_async_remote_copy(
            src_ref=w.at[which, pl.ds(pl.multiple_of(start, 16), size)],
            dst_ref=w.at[which, pl.ds(pl.multiple_of(start + units, 16), size)],
            send_sem=w_send.at[i],
            recv_sem=w_recv.at[i],
            device_id=partner,
            device_id_type=MESH,
        )

    def hand_on(i):
        which, start, size = ((core, 0, big), (core, big, small), (2, core * big, small))[i]
        at = pl.ds(pl.multiple_of(start + units, 16), size)
        return pltpu.make_async_remote_copy(
            src_ref=w.at[which, at],
            dst_ref=w.at[which, at],
            send_sem=f_send.at[i],
            recv_sem=f_recv.at[i],
            device_id=sibling,
            device_id_type=MESH,
        )

    def arrived_weights(i):
        from_partner(i).wait_recv()
        hand_on(i).start()

    pass_on(0, lambda way: first[way][0])
    pass_on(0, lambda way: first[way][1])
    pass_on(0, lambda way: second[way][0])
    for load in loads[1:]:
        load.wait()
    for i in range(3):
        from_partner(i).start()

    pass_on(1, lambda way: first[way][0])
    pass_on(1, lambda way: first[way][1])
    pass_on(0, lambda way: second[way][1])
    arrived_weights(0)
    pass_on(2, lambda way: first[way][0])
    pass_on(2, lambda way: first[way][1])
    pass_on(1, lambda way: second[way][0])
    arrived_weights(1)
    pass_on(3, lambda way: first[way][0])
    pass_on(3, lambda way: first[way][1])
    pass_on(1, lambda way: second[way][1])
    arrived_weights(2)
    pass_on(2, lambda way: second[way][0])
    pass_on(2, lambda way: second[way][1])
    for i in range(3):
        hand_on(i).wait_recv()

    def work(*blocks):
        tile = jnp.concatenate([x[s, a : a + n] for s, a, n in blocks], axis=0)
        gate = lax.dot_general(tile, w[0], ROWS_BY_COLS, preferred_element_type=F32)
        up = lax.dot_general(tile, w[1], ROWS_BY_COLS, preferred_element_type=F32)
        hidden = (gate / (1.0 + jnp.exp(-gate)) * up).astype(BF16)
        result = jnp.dot(hidden, w[2], preferred_element_type=F32)
        row = 0
        for s, a, n in blocks:
            acc[s, a : a + n] = result[row : row + n]
            row += n

    def reduce(way, step, piece):
        at = pl.ds(piece * part, part)
        return pltpu.make_async_remote_copy(
            src_ref=sums.at[way, step, at],
            dst_ref=came.at[way, step, at],
            send_sem=rs_send.at[way, step, piece],
            recv_sem=rs_recv.at[way, step, piece],
            device_id=towards[way],
            device_id_type=MESH,
        )

    def send_sum(way, step, piece, add):
        slot = 4 + step if way == UP else 4 - step
        at = pl.ds(piece * part, part)
        value = acc[slot, at]
        if add:
            reduce(way, step - 1, piece).wait_recv()
            value = value + came[way, step - 1, at].astype(F32)
        sums[way, step, at] = value.astype(BF16)
        reduce(way, step, piece).start()

    work((0, 0, rows), (1, 0, rows), (7, 0, rows))
    for way in (UP, DOWN):
        for piece in first[way]:
            gather(way, 3, piece).wait_recv()
    work((3, half, half), (4, 0, rows), (5, 0, half))
    for i in (0, 1):
        for way in (UP, DOWN):
            send_sum(way, 0, first[way][i], False)
    for i in (0, 1):
        for way in (UP, DOWN):
            send_sum(way, 1, second[way][i], False)
    for way in (UP, DOWN):
        for piece in second[way]:
            gather(way, 2, piece).wait_recv()
    work((3, 0, half), (5, half, half), (2, 0, rows), (6, 0, rows))
    for i in (0, 1):
        for way in (UP, DOWN):
            send_sum(way, 1, first[way][i], True)
    for step in (2, 3):
        for order in (second, first):
            for i in (0, 1):
                for way in (UP, DOWN):
                    send_sum(way, step, order[way][i], True)
    for order in (second, first):
        for i in (0, 1):
            for way in (UP, DOWN):
                reduce(way, 3, order[way][i]).wait_recv()
    out_ref[...] = (acc[0] + came[UP, 3].astype(F32) + came[DOWN, 3].astype(F32)).astype(BF16)

    for way in (UP, DOWN):
        for hop in range(4):
            for piece in range(PIECES):
                if hop < 3 or piece in first[way]:
                    gather(way, hop, piece).wait_send()
                if hop > 0 or piece in first[way]:
                    reduce(way, hop, piece).wait_send()
    for i in range(3):
        from_partner(i).wait_send()
        hand_on(i).wait_send()


def shards(tokens, smooth_scale, gate_weight, up_weight, down_weight):
    rows, width = tokens.shape
    units = gate_weight.shape[0]
    here = pl.BlockSpec(memory_space=pl.ANY)
    dma = pltpu.SemaphoreType.DMA
    return pl.pallas_call(
        kernel,
        out_shape=jax.ShapeDtypeStruct((rows, width), BF16),
        in_specs=[here, pl.BlockSpec(memory_space=pltpu.VMEM), here, here, here],
        out_specs=pl.BlockSpec(memory_space=pltpu.VMEM),
        scratch_shapes=[
            pltpu.VMEM((rows, width), BF16),
            pltpu.VMEM((8, rows, width), BF16),
            pltpu.VMEM((3, 2 * units, width), BF16),
            pltpu.VMEM((8, rows, width), F32),
            pltpu.VMEM((2, 4, rows, width), BF16),
            pltpu.VMEM((2, 4, rows, width), BF16),
            dma((4,)),
            dma((2, 4, PIECES)),
            dma((2, 4, PIECES)),
            dma((2, 4, PIECES)),
            dma((2, 4, PIECES)),
            dma((3,)),
            dma((3,)),
            dma((3,)),
            dma((3,)),
        ],
        compiler_params=pltpu.CompilerParams(
            collective_id=0, has_side_effects=True, vmem_limit_bytes=48 << 20
        ),
    )(tokens, smooth_scale.reshape(1, width), gate_weight, up_weight, down_weight)


def solution(mesh):
    return jax.shard_map(
        shards,
        mesh=mesh,
        in_specs=(
            P(("dp", "tensor"), None),
            P(),
            P("tensor", None),
            P("tensor", None),
            P("tensor", None),
        ),
        out_specs=P(("dp", "tensor"), None),
        check_vma=False,
    )
```

```python
import jax
import jax.numpy as jnp
from jax import lax
from jax.experimental import pallas as pl
from jax.experimental.pallas import tpu as pltpu
from jax.sharding import PartitionSpec as P

MESH = pl.DeviceIdType.MESH
BF16, F32 = jnp.bfloat16, jnp.float32
ROWS_BY_COLS = (((1,), (1,)), ((), ()))
UP, DOWN = 0, 1
PIECES = 4


def kernel(
    tokens_ref, scale_ref, gate_ref, up_ref, down_ref, out_ref,
    raw, scale, x, w, acc, sums, came,
    load_sem, ag_send, ag_recv, rs_send, rs_recv, w_send, w_recv, f_send, f_recv,
):
    dp, t = lax.axis_index("dp"), lax.axis_index("tensor")
    core, x_hi = lax.rem(dp, 2), lax.rem(dp // 2, 2)
    other_t = t + 1 - 2 * lax.rem(t, 2)
    towards = ((dp, lax.rem(t + 2, 16)), (dp, lax.rem(t + 14, 16)))
    sibling = (dp + 1 - 2 * core, t)
    partner = (dp + core * (2 - 4 * x_hi), other_t)

    rows = tokens_ref.shape[0]
    part = rows // PIECES
    half = rows // 2
    units = gate_ref.shape[0]
    big = (units // 2 + 15) // 16 * 16
    small = units - big

    loads = [
        pltpu.make_async_copy(tokens_ref, raw, load_sem.at[0]),
        pltpu.make_async_copy(scale_ref, scale, load_sem.at[1]),
    ]
    for i, ref in enumerate((gate_ref, up_ref, down_ref)):
        loads.append(pltpu.make_async_copy(ref, w.at[i, pl.ds(0, units)], load_sem.at[i + 2]))
    for load in loads:
        load.start()

    barrier = pltpu.get_barrier_semaphore()
    for device in (*towards, sibling, partner):
        pl.semaphore_signal(barrier, inc=1, device_id=device, device_id_type=MESH)

    loads[0].wait()
    loads[1].wait()
    x[0] = (raw[...].astype(F32) / scale[...][None, :]).astype(BF16)
    pl.semaphore_wait(barrier, 4)

    def gather(way, hop, piece):
        here = hop if way == UP else (8 - hop) % 8
        there = hop + 1 if way == UP else 7 - hop
        at = pl.ds(piece * part, part)
        return pltpu.make_async_remote_copy(
            src_ref=x.at[here, at],
            dst_ref=x.at[there, at],
            send_sem=ag_send.at[way, hop, piece],
            recv_sem=ag_recv.at[way, hop, piece],
            device_id=towards[way],
            device_id_type=MESH,
        )

    first = ((2, 3), (0, 1))
    second = ((0, 1), (2, 3))

    def pass_on(hop, piece_of):
        for way in (UP, DOWN):
            if hop:
                gather(way, hop - 1, piece_of(way)).wait_recv()
            gather(way, hop, piece_of(way)).start()

    def from_partner(i):
        which, start, size = ((core, 0, big), (core, big, small), (2, core * small, big))[i]
        return pltpu.make_async_remote_copy(
            src_ref=w.at[which, pl.ds(pl.multiple_of(start, 16), size)],
            dst_ref=w.at[which, pl.ds(pl.multiple_of(start + units, 16), size)],
            send_sem=w_send.at[i],
            recv_sem=w_recv.at[i],
            device_id=partner,
            device_id_type=MESH,
        )

    def hand_on(i):
        which, start, size = ((core, 0, big), (core, big, small), (2, core * big, small))[i]
        at = pl.ds(pl.multiple_of(start + units, 16), size)
        return pltpu.make_async_remote_copy(
            src_ref=w.at[which, at],
            dst_ref=w.at[which, at],
            send_sem=f_send.at[i],
            recv_sem=f_recv.at[i],
            device_id=sibling,
            device_id_type=MESH,
        )

    def arrived_weights(i):
        from_partner(i).wait_recv()
        hand_on(i).start()

    pass_on(0, lambda way: first[way][0])
    pass_on(0, lambda way: first[way][1])
    pass_on(0, lambda way: second[way][0])
    for load in loads[2:]:
        load.wait()
    for i in range(3):
        from_partner(i).start()

    pass_on(1, lambda way: first[way][0])
    pass_on(1, lambda way: first[way][1])
    pass_on(0, lambda way: second[way][1])
    arrived_weights(0)
    pass_on(2, lambda way: first[way][0])
    pass_on(2, lambda way: first[way][1])
    pass_on(1, lambda way: second[way][0])
    arrived_weights(1)
    pass_on(3, lambda way: first[way][0])
    pass_on(3, lambda way: first[way][1])
    pass_on(1, lambda way: second[way][1])
    arrived_weights(2)
    pass_on(2, lambda way: second[way][0])
    pass_on(2, lambda way: second[way][1])
    for i in range(3):
        hand_on(i).wait_recv()

    def work(*blocks):
        tile = jnp.concatenate([x[s, a : a + n] for s, a, n in blocks], axis=0)
        gate = lax.dot_general(tile, w[0], ROWS_BY_COLS, preferred_element_type=F32)
        up = lax.dot_general(tile, w[1], ROWS_BY_COLS, preferred_element_type=F32)
        hidden = (gate / (1.0 + jnp.exp(-gate)) * up).astype(BF16)
        result = jnp.dot(hidden, w[2], preferred_element_type=F32)
        row = 0
        for s, a, n in blocks:
            acc[s, a : a + n] = result[row : row + n]
            row += n

    def reduce(way, step, piece):
        at = pl.ds(piece * part, part)
        return pltpu.make_async_remote_copy(
            src_ref=sums.at[way, step, at],
            dst_ref=came.at[way, step, at],
            send_sem=rs_send.at[way, step, piece],
            recv_sem=rs_recv.at[way, step, piece],
            device_id=towards[way],
            device_id_type=MESH,
        )

    def send_sum(way, step, piece, add):
        slot = 4 + step if way == UP else 4 - step
        at = pl.ds(piece * part, part)
        value = acc[slot, at]
        if add:
            reduce(way, step - 1, piece).wait_recv()
            value = value + came[way, step - 1, at].astype(F32)
        sums[way, step, at] = value.astype(BF16)
        reduce(way, step, piece).start()

    work((0, 0, rows), (1, 0, rows), (7, 0, rows))
    for way in (UP, DOWN):
        for piece in first[way]:
            gather(way, 3, piece).wait_recv()
    work((3, half, half), (4, 0, rows), (5, 0, half))
    for i in (0, 1):
        for way in (UP, DOWN):
            send_sum(way, 0, first[way][i], False)
    for i in (0, 1):
        for way in (UP, DOWN):
            send_sum(way, 1, second[way][i], False)
    for way in (UP, DOWN):
        for piece in second[way]:
            gather(way, 2, piece).wait_recv()
    work((3, 0, half), (5, half, half), (2, 0, rows), (6, 0, rows))
    for i in (0, 1):
        for way in (UP, DOWN):
            send_sum(way, 1, first[way][i], True)
    for step in (2, 3):
        for order in (second, first):
            for i in (0, 1):
                for way in (UP, DOWN):
                    send_sum(way, step, order[way][i], True)
    for order in (second, first):
        for i in (0, 1):
            for way in (UP, DOWN):
                reduce(way, 3, order[way][i]).wait_recv()
    out_ref[...] = (acc[0] + came[UP, 3].astype(F32) + came[DOWN, 3].astype(F32)).astype(BF16)

    for way in (UP, DOWN):
        for hop in range(4):
            for piece in range(PIECES):
                if hop < 3 or piece in first[way]:
                    gather(way, hop, piece).wait_send()
                if hop > 0 or piece in first[way]:
                    reduce(way, hop, piece).wait_send()
    for i in range(3):
        from_partner(i).wait_send()
        hand_on(i).wait_send()


def shards(tokens, smooth_scale, gate_weight, up_weight, down_weight):
    rows, width = tokens.shape
    units = gate_weight.shape[0]
    here = pl.BlockSpec(memory_space=pltpu.HBM)
    dma = pltpu.SemaphoreType.DMA
    return pl.pallas_call(
        kernel,
        out_shape=jax.ShapeDtypeStruct((rows, width), BF16),
        in_specs=[here] * 5,
        out_specs=pl.BlockSpec(memory_space=pltpu.VMEM),
        scratch_shapes=[
            pltpu.VMEM((rows, width), BF16),
            pltpu.VMEM((width,), F32),
            pltpu.VMEM((8, rows, width), BF16),
            pltpu.VMEM((3, 2 * units, width), BF16),
            pltpu.VMEM((8, rows, width), F32),
            pltpu.VMEM((2, 4, rows, width), BF16),
            pltpu.VMEM((2, 4, rows, width), BF16),
            dma((5,)),
            dma((2, 4, PIECES)),
            dma((2, 4, PIECES)),
            dma((2, 4, PIECES)),
            dma((2, 4, PIECES)),
            dma((3,)),
            dma((3,)),
            dma((3,)),
            dma((3,)),
        ],
        compiler_params=pltpu.CompilerParams(
            collective_id=0, has_side_effects=True, vmem_limit_bytes=60 << 20
        ),
    )(tokens, smooth_scale, gate_weight, up_weight, down_weight)


def solution(mesh):
    return jax.shard_map(
        shards,
        mesh=mesh,
        in_specs=(
            P(("dp", "tensor"), None),
            P(),
            P("tensor", None),
            P("tensor", None),
            P("tensor", None),
        ),
        out_specs=P(("dp", "tensor"), None),
        check_vma=False,
    )
```

```python
import jax
import jax.numpy as jnp
from jax import lax
from jax.experimental import pallas as pl
from jax.experimental.pallas import tpu as pltpu
from jax.sharding import PartitionSpec as P

MESH = pl.DeviceIdType.MESH
BF16, F32 = jnp.bfloat16, jnp.float32
ROWS_BY_COLS = (((1,), (1,)), ((), ()))
UP, DOWN = 0, 1
PIECES = 4


def kernel(
    tokens_ref, scale_ref, gate_ref, up_ref, down_ref, out_ref,
    raw, scale, x, w, acc, sums, came,
    load_sem, ag_send, ag_recv, rs_send, rs_recv, w_send, w_recv, f_send, f_recv,
):
    dp, t = lax.axis_index("dp"), lax.axis_index("tensor")
    core, x_hi = lax.rem(dp, 2), lax.rem(dp // 2, 2)
    other_t = t + 1 - 2 * lax.rem(t, 2)
    towards = ((dp, lax.rem(t + 2, 16)), (dp, lax.rem(t + 14, 16)))
    sibling = (dp + 1 - 2 * core, t)
    partner = (dp + core * (2 - 4 * x_hi), other_t)

    rows = tokens_ref.shape[0]
    part = rows // PIECES
    half = rows // 2
    units = gate_ref.shape[0]
    big = (units // 2 + 15) // 16 * 16
    small = units - big

    order = (0, 2, 1, 3)
    loads = [pltpu.make_async_copy(scale_ref, scale, load_sem.at[0])]
    for i in order:
        at = pl.ds(i * part, part)
        loads.append(pltpu.make_async_copy(tokens_ref.at[at], raw.at[at], load_sem.at[1 + i]))
    for i, ref in enumerate((gate_ref, up_ref, down_ref)):
        loads.append(pltpu.make_async_copy(ref, w.at[i, pl.ds(0, units)], load_sem.at[5 + i]))
    barrier = pltpu.get_barrier_semaphore()
    for device in (*towards, sibling, partner):
        pl.semaphore_signal(barrier, inc=1, device_id=device, device_id_type=MESH)
    for load in loads:
        load.start()

    loads[0].wait()
    for i, load in zip(order, loads[1:5], strict=True):
        load.wait()
        at = pl.ds(i * part, part)
        x[0, at] = (raw[at].astype(F32) / scale[...][None, :]).astype(BF16)
    pl.semaphore_wait(barrier, 4)

    def gather(way, hop, piece):
        here = hop if way == UP else (8 - hop) % 8
        there = hop + 1 if way == UP else 7 - hop
        at = pl.ds(piece * part, part)
        return pltpu.make_async_remote_copy(
            src_ref=x.at[here, at],
            dst_ref=x.at[there, at],
            send_sem=ag_send.at[way, hop, piece],
            recv_sem=ag_recv.at[way, hop, piece],
            device_id=towards[way],
            device_id_type=MESH,
        )

    first = ((2, 3), (0, 1))
    second = ((0, 1), (2, 3))

    def pass_on(hop, piece_of):
        for way in (UP, DOWN):
            if hop:
                gather(way, hop - 1, piece_of(way)).wait_recv()
            gather(way, hop, piece_of(way)).start()

    def from_partner(i):
        which, start, size = ((core, 0, big), (core, big, small), (2, core * small, big))[i]
        return pltpu.make_async_remote_copy(
            src_ref=w.at[which, pl.ds(pl.multiple_of(start, 16), size)],
            dst_ref=w.at[which, pl.ds(pl.multiple_of(start + units, 16), size)],
            send_sem=w_send.at[i],
            recv_sem=w_recv.at[i],
            device_id=partner,
            device_id_type=MESH,
        )

    def hand_on(i):
        which, start, size = ((core, 0, big), (core, big, small), (2, core * big, small))[i]
        at = pl.ds(pl.multiple_of(start + units, 16), size)
        return pltpu.make_async_remote_copy(
            src_ref=w.at[which, at],
            dst_ref=w.at[which, at],
            send_sem=f_send.at[i],
            recv_sem=f_recv.at[i],
            device_id=sibling,
            device_id_type=MESH,
        )

    def arrived_weights(i):
        from_partner(i).wait_recv()
        hand_on(i).start()

    pass_on(0, lambda way: first[way][0])
    pass_on(0, lambda way: first[way][1])
    pass_on(0, lambda way: second[way][0])
    for load in loads[5:]:
        load.wait()
    for i in range(3):
        from_partner(i).start()

    pass_on(1, lambda way: first[way][0])
    pass_on(1, lambda way: first[way][1])
    pass_on(0, lambda way: second[way][1])
    arrived_weights(0)
    pass_on(2, lambda way: first[way][0])
    pass_on(2, lambda way: first[way][1])
    pass_on(1, lambda way: second[way][0])
    arrived_weights(1)
    pass_on(3, lambda way: first[way][0])
    pass_on(3, lambda way: first[way][1])
    pass_on(1, lambda way: second[way][1])
    arrived_weights(2)
    for i in range(3):
        hand_on(i).wait_recv()

    def work(*blocks):
        tile = jnp.concatenate([x[s, a : a + n] for s, a, n in blocks], axis=0)
        gate = lax.dot_general(tile, w[0], ROWS_BY_COLS, preferred_element_type=F32)
        up = lax.dot_general(tile, w[1], ROWS_BY_COLS, preferred_element_type=F32)
        hidden = (gate / (1.0 + jnp.exp(-gate)) * up).astype(BF16)
        result = jnp.dot(hidden, w[2], preferred_element_type=F32)
        row = 0
        for s, a, n in blocks:
            acc[s, a : a + n] = result[row : row + n]
            row += n

    def reduce(way, step, piece):
        at = pl.ds(piece * part, part)
        return pltpu.make_async_remote_copy(
            src_ref=sums.at[way, step, at],
            dst_ref=came.at[way, step, at],
            send_sem=rs_send.at[way, step, piece],
            recv_sem=rs_recv.at[way, step, piece],
            device_id=towards[way],
            device_id_type=MESH,
        )

    def send_sum(way, step, piece, add):
        slot = 4 + step if way == UP else 4 - step
        at = pl.ds(piece * part, part)
        value = acc[slot, at]
        if add:
            reduce(way, step - 1, piece).wait_recv()
            value = value + came[way, step - 1, at].astype(F32)
        sums[way, step, at] = value.astype(BF16)
        reduce(way, step, piece).start()

    work((0, 0, rows), (1, 0, rows), (7, 0, rows))
    pass_on(2, lambda way: second[way][0])
    for way in (UP, DOWN):
        for piece in first[way]:
            gather(way, 3, piece).wait_recv()
    pass_on(2, lambda way: second[way][1])
    work((3, half, half), (4, 0, rows), (5, 0, half))
    for i in (0, 1):
        for way in (UP, DOWN):
            send_sum(way, 0, first[way][i], False)
    for i in (0, 1):
        for way in (UP, DOWN):
            send_sum(way, 1, second[way][i], False)
    for way in (UP, DOWN):
        for piece in second[way]:
            gather(way, 2, piece).wait_recv()
    work((3, 0, half), (5, half, half), (2, 0, rows), (6, 0, rows))
    for i in (0, 1):
        for way in (UP, DOWN):
            send_sum(way, 1, first[way][i], True)
    for step in (2, 3):
        for order in (second, first):
            for i in (0, 1):
                for way in (UP, DOWN):
                    send_sum(way, step, order[way][i], True)
    for order in (second, first):
        for i in (0, 1):
            for way in (UP, DOWN):
                piece = order[way][i]
                at = pl.ds(piece * part, part)
                reduce(way, 3, piece).wait_recv()
                value = acc[0, at] + came[way, 3, at].astype(F32)
                if order is second:
                    acc[0, at] = value
                else:
                    out_ref[at] = value.astype(BF16)

    for way in (UP, DOWN):
        for hop in range(4):
            for piece in range(PIECES):
                if hop < 3 or piece in first[way]:
                    gather(way, hop, piece).wait_send()
                if hop > 0 or piece in first[way]:
                    reduce(way, hop, piece).wait_send()
    for i in range(3):
        from_partner(i).wait_send()
        hand_on(i).wait_send()


def shards(tokens, smooth_scale, gate_weight, up_weight, down_weight):
    rows, width = tokens.shape
    units = gate_weight.shape[0]
    here = pl.BlockSpec(memory_space=pltpu.HBM)
    operands = (tokens, smooth_scale, gate_weight, up_weight, down_weight)
    dma = pltpu.SemaphoreType.DMA
    return pl.pallas_call(
        kernel,
        out_shape=pltpu.VMEM((rows, width), BF16),
        in_specs=[here] * 5,
        out_specs=pl.BlockSpec(memory_space=pltpu.VMEM),
        scratch_shapes=[
            pltpu.VMEM((rows, width), BF16),
            pltpu.VMEM((width,), F32),
            pltpu.VMEM((8, rows, width), BF16),
            pltpu.VMEM((3, 2 * units, width), BF16),
            pltpu.VMEM((8, rows, width), F32),
            pltpu.VMEM((2, 4, rows, width), BF16),
            pltpu.VMEM((2, 4, rows, width), BF16),
            dma((8,)),
            dma((2, 4, PIECES)),
            dma((2, 4, PIECES)),
            dma((2, 4, PIECES)),
            dma((2, 4, PIECES)),
            dma((3,)),
            dma((3,)),
            dma((3,)),
            dma((3,)),
        ],
        compiler_params=pltpu.CompilerParams(
            collective_id=0, has_side_effects=True, vmem_limit_bytes=48 << 20
        ),
    )(*(pltpu.with_memory_space_constraint(o, pltpu.HBM) for o in operands))


def solution(mesh):
    return jax.shard_map(
        shards,
        mesh=mesh,
        in_specs=(
            P(("dp", "tensor"), None),
            P(),
            P("tensor", None),
            P("tensor", None),
            P("tensor", None),
        ),
        out_specs=P(("dp", "tensor"), None),
        check_vma=False,
    )
```

```python
import jax
import jax.numpy as jnp
from jax import lax
from jax.experimental import pallas as pl
from jax.experimental.pallas import tpu as pltpu
from jax.sharding import PartitionSpec as P

MESH = pl.DeviceIdType.MESH
BF16, F32 = jnp.bfloat16, jnp.float32
ROWS_BY_COLS = (((1,), (1,)), ((), ()))
UP, DOWN = 0, 1
PIECES = 4


def kernel(
    tokens_ref, scale_ref, gate_ref, up_ref, down_ref, out_ref,
    raw, scale, x, w, acc, sums, came,
    load_sem, ag_send, ag_recv, rs_send, rs_recv, w_load, w_send, w_recv, f_recv,
):
    dp, t = lax.axis_index("dp"), lax.axis_index("tensor")
    core, x_hi = lax.rem(dp, 2), lax.rem(dp // 2, 2)
    other_t = t + 1 - 2 * lax.rem(t, 2)
    towards = ((dp, lax.rem(t + 2, 16)), (dp, lax.rem(t + 14, 16)))
    sibling = (dp + 1 - 2 * core, t)
    partner = (dp + core * (2 - 4 * x_hi), other_t)

    rows = tokens_ref.shape[0]
    part = rows // PIECES
    half = rows // 2
    units = gate_ref.shape[0]
    big = (units // 2 + 15) // 16 * 16
    small = units - big

    loads = [
        pltpu.make_async_copy(scale_ref, scale, load_sem.at[0]),
        pltpu.make_async_copy(tokens_ref, raw, load_sem.at[1]),
    ]
    for i, ref in enumerate((gate_ref, up_ref, down_ref)):
        loads.append(pltpu.make_async_copy(ref, w.at[i, pl.ds(0, units)], w_load))
    own = w.at[:, pl.ds(0, units)]
    barrier = pltpu.get_barrier_semaphore()
    for device in (*towards, sibling, partner):
        pl.semaphore_signal(barrier, inc=1, device_id=device, device_id_type=MESH)
    for load in loads:
        load.start()
    loads[0].wait()
    loads[1].wait()
    x[0] = (raw[...].astype(F32) / scale[...][None, :]).astype(BF16)
    pl.semaphore_wait(barrier, 4)

    far = ((2, 3), (0, 1))
    near = ((0, 1), (2, 3))

    def gather(way, hop, piece):
        here = hop if way == UP else (8 - hop) % 8
        there = hop + 1 if way == UP else 7 - hop
        at = pl.ds(piece * part, part)
        slot = 4 * hop + (far[way] + near[way]).index(piece)
        return pltpu.make_async_remote_copy(
            src_ref=x.at[here, at],
            dst_ref=x.at[there, at],
            send_sem=ag_send,
            recv_sem=ag_recv.at[way, slot],
            device_id=towards[way],
            device_id_type=MESH,
        )

    def pass_on(hop, which, i):
        for way in (UP, DOWN):
            if hop:
                gather(way, hop - 1, which[way][i]).wait_recv()
            gather(way, hop, which[way][i]).start()

    def from_partner(i):
        which, start, size = ((core, 0, big), (core, big, small), (2, core * small, big))[i]
        return pltpu.make_async_remote_copy(
            src_ref=w.at[which, pl.ds(pl.multiple_of(start, 16), size)],
            dst_ref=w.at[which, pl.ds(pl.multiple_of(start + units, 16), size)],
            send_sem=w_send,
            recv_sem=w_recv.at[i],
            device_id=partner,
            device_id_type=MESH,
        )

    def hand_on(i):
        which, start, size = ((core, 0, big), (core, big, small), (2, core * big, small))[i]
        at = pl.ds(pl.multiple_of(start + units, 16), size)
        return pltpu.make_async_remote_copy(
            src_ref=w.at[which, at],
            dst_ref=w.at[which, at],
            send_sem=w_send,
            recv_sem=f_recv.at[i],
            device_id=sibling,
            device_id_type=MESH,
        )

    def arrived_weights(i):
        from_partner(i).wait_recv()
        hand_on(i).start()

    def work(*blocks):
        tile = jnp.concatenate([x[s, a : a + n] for s, a, n in blocks], axis=0)
        gate = lax.dot_general(tile, w[0], ROWS_BY_COLS, preferred_element_type=F32)
        up = lax.dot_general(tile, w[1], ROWS_BY_COLS, preferred_element_type=F32)
        hidden = (gate / (1.0 + jnp.exp(-gate)) * up).astype(BF16)
        result = jnp.dot(hidden, w[2], preferred_element_type=F32)
        row = 0
        for s, a, n in blocks:
            acc[s, a : a + n] = result[row : row + n]
            row += n

    def reduce(way, step, piece):
        at = pl.ds(piece * part, part)
        slot = 4 * step + far[way].index(piece) if piece in far[way] else 4 * step - 2 + near[way].index(piece)
        return pltpu.make_async_remote_copy(
            src_ref=sums.at[4 * way + step, at],
            dst_ref=came.at[4 * way + step, at],
            send_sem=rs_send,
            recv_sem=rs_recv.at[way, slot],
            device_id=towards[way],
            device_id_type=MESH,
        )

    def send_sum(step, which, i):
        for way in (UP, DOWN):
            piece = which[way][i]
            at = pl.ds(piece * part, part)
            value = acc[4 + step if way == UP else 4 - step, at]
            if step > 1 or (step == 1 and which is far):
                reduce(way, step - 1, piece).wait_recv()
                value = value + came[4 * way + step - 1, at].astype(F32)
            sums[4 * way + step, at] = value.astype(BF16)
            reduce(way, step, piece).start()

    pass_on(0, far, 0)
    pass_on(0, far, 1)
    pass_on(0, near, 0)
    pltpu.make_async_copy(own, own, w_load).wait()
    for i in range(3):
        from_partner(i).start()
    pass_on(1, far, 0)
    pass_on(1, far, 1)
    pass_on(0, near, 1)
    arrived_weights(0)
    pass_on(2, far, 0)
    pass_on(2, far, 1)
    pass_on(1, near, 0)
    arrived_weights(1)
    pass_on(3, far, 0)
    arrived_weights(2)
    pass_on(3, far, 1)
    pass_on(1, near, 1)
    for i in range(3):
        hand_on(i).wait_recv()
    work((3, half, half), (5, 0, half))
    pass_on(2, near, 0)
    send_sum(1, near, 0)
    work((0, 0, rows), (1, 0, rows), (7, 0, rows))
    for way in (UP, DOWN):
        for piece in far[way]:
            gather(way, 3, piece).wait_recv()
    work((4, 0, rows))
    pass_on(2, near, 1)
    send_sum(0, far, 0)
    send_sum(0, far, 1)
    send_sum(1, near, 1)
    work((2, 0, rows), (6, 0, rows))
    for way in (UP, DOWN):
        for piece in near[way]:
            gather(way, 2, piece).wait_recv()
    work((3, 0, half), (5, half, half))
    send_sum(1, far, 0)
    send_sum(1, far, 1)
    for step in (2, 3):
        for which in (near, far):
            for i in (0, 1):
                send_sum(step, which, i)
    for which in (near, far):
        for i in (0, 1):
            for way in (UP, DOWN):
                piece = which[way][i]
                at = pl.ds(piece * part, part)
                reduce(way, 3, piece).wait_recv()
                value = acc[0, at] + came[4 * way + 3, at].astype(F32)
                if which is near:
                    acc[0, at] = value
                else:
                    out_ref[at] = value.astype(BF16)

    for sent, sem in ((x.at[pl.ds(0, 7)], ag_send), (sums.at[pl.ds(0, 7)], rs_send), (own, w_send)):
        pltpu.make_async_copy(sent, sent, sem).wait()


def shards(tokens, smooth_scale, gate_weight, up_weight, down_weight):
    rows, width = tokens.shape
    units = gate_weight.shape[0]
    here = pl.BlockSpec(memory_space=pltpu.HBM)
    operands = (tokens, smooth_scale, gate_weight, up_weight, down_weight)
    dma = pltpu.SemaphoreType.DMA
    return pl.pallas_call(
        kernel,
        out_shape=pltpu.VMEM((rows, width), BF16),
        in_specs=[here] * 5,
        out_specs=pl.BlockSpec(memory_space=pltpu.VMEM),
        scratch_shapes=[
            pltpu.VMEM((rows, width), BF16),
            pltpu.VMEM((width,), F32),
            pltpu.VMEM((8, rows, width), BF16),
            pltpu.VMEM((3, 2 * units, width), BF16),
            pltpu.VMEM((8, rows, width), F32),
            pltpu.VMEM((8, rows, width), BF16),
            pltpu.VMEM((8, rows, width), BF16),
            dma((2,)),
            dma,
            dma((2, 14)),
            dma,
            dma((2, 14)),
            dma,
            dma,
            dma((3,)),
            dma((3,)),
        ],
        compiler_params=pltpu.CompilerParams(
            collective_id=0, has_side_effects=True, vmem_limit_bytes=48 << 20
        ),
    )(*(pltpu.with_memory_space_constraint(o, pltpu.HBM) for o in operands))


def solution(mesh):
    return jax.shard_map(
        shards,
        mesh=mesh,
        in_specs=(
            P(("dp", "tensor"), None),
            P(),
            P("tensor", None),
            P("tensor", None),
            P("tensor", None),
        ),
        out_specs=P(("dp", "tensor"), None),
        check_vma=False,
    )
```

```python
import jax
import jax.numpy as jnp
from jax import lax
from jax.experimental import pallas as pl
from jax.experimental.pallas import tpu as pltpu
from jax.sharding import PartitionSpec as P

MESH = pl.DeviceIdType.MESH
BF16, F32 = jnp.bfloat16, jnp.float32
ROWS_BY_COLS = (((1,), (1,)), ((), ()))
UP, DOWN = 0, 1
PIECES = 4


def kernel(
    tokens_ref, scale_ref, gate_ref, up_ref, down_ref, out_ref,
    raw, scale, x, w, acc, sums, came,
    load_sem, ag_send, rs_send, recv, w_load, w_send, w_recv, f_recv,
):
    dp, t = lax.axis_index("dp"), lax.axis_index("tensor")
    core, x_hi, x_lo = dp & 1, (dp >> 1) & 1, t & 1
    other_t = t + 1 - 2 * x_lo
    towards = ((dp, (t + 2) & 15), (dp, (t + 14) & 15))
    sibling = (dp + 1 - 2 * core, t)
    partner = (dp + core * (2 - 4 * x_hi), other_t)
    barrier = pltpu.get_barrier_semaphore()
    for device in (*towards, sibling, partner):
        pl.semaphore_signal(barrier, inc=1, device_id=device, device_id_type=MESH)

    rows = tokens_ref.shape[0]
    part = rows // PIECES
    half = rows // 2
    units = gate_ref.shape[0]
    big = (units // 2 + 15) // 16 * 16
    small = units - big

    own = w.at[:, pl.ds(0, units)]
    loads = [
        pltpu.make_async_copy(tokens_ref, raw, load_sem.at[0]),
        pltpu.make_async_copy(scale_ref, scale, load_sem.at[1]),
    ]
    for load in loads:
        load.start()

    for load in loads:
        load.wait()
    for i, ref in enumerate((gate_ref, up_ref, down_ref)):
        pltpu.make_async_copy(ref, w.at[i, pl.ds(0, units)], w_load).start()
    inverse = 1.0 / scale[...][None, :]
    x[0] = (raw[...].astype(F32) * inverse).astype(BF16)
    pl.semaphore_wait(barrier, 4)

    far = ((2, 3), (0, 1))
    near = ((0, 1), (2, 3))

    def gather(way, hop, piece):
        here = hop if way == UP else (8 - hop) % 8
        there = hop + 1 if way == UP else 7 - hop
        at = pl.ds(piece * part, part)
        slot = 4 * hop + (far[way] + near[way]).index(piece)
        return pltpu.make_async_remote_copy(
            src_ref=x.at[here, at],
            dst_ref=x.at[there, at],
            send_sem=ag_send,
            recv_sem=recv.at[way, slot],
            device_id=towards[way],
            device_id_type=MESH,
        )

    def pass_on(hop, which, i):
        for way in (UP, DOWN):
            if hop:
                gather(way, hop - 1, which[way][i]).wait_recv()
            gather(way, hop, which[way][i]).start()

    def from_partner(i):
        which, start, size = ((core, 0, big), (core, big, small), (2, core * small, big))[i]
        return pltpu.make_async_remote_copy(
            src_ref=w.at[which, pl.ds(pl.multiple_of(start, 16), size)],
            dst_ref=w.at[which, pl.ds(pl.multiple_of(start + units, 16), size)],
            send_sem=w_send,
            recv_sem=w_recv.at[i],
            device_id=partner,
            device_id_type=MESH,
        )

    def hand_on(i):
        which, start, size = ((core, 0, big), (core, big, small), (2, core * big, small))[i]
        at = pl.ds(pl.multiple_of(start + units, 16), size)
        return pltpu.make_async_remote_copy(
            src_ref=w.at[which, at],
            dst_ref=w.at[which, at],
            send_sem=w_send,
            recv_sem=f_recv.at[i],
            device_id=sibling,
            device_id_type=MESH,
        )

    def arrived_weights(i):
        from_partner(i).wait_recv()
        hand_on(i).start()

    def work(*blocks):
        tile = jnp.concatenate([x[s, a : a + n] for s, a, n in blocks], axis=0)
        gate = lax.dot_general(tile, w[0], ROWS_BY_COLS, preferred_element_type=F32)
        up = lax.dot_general(tile, w[1], ROWS_BY_COLS, preferred_element_type=F32)
        hidden = (gate / (1.0 + jnp.exp(-gate)) * up).astype(BF16)
        result = jnp.dot(hidden, w[2], preferred_element_type=F32)
        row = 0
        for s, a, n in blocks:
            acc[s, a : a + n] = result[row : row + n]
            row += n

    takes_over = {(0, far): 4, (1, near): 0, (1, far): 2, (2, near): 8, (2, far): 6, (3, near): 10, (3, far): 12}

    def reduce(way, step, piece):
        at = pl.ds(piece * part, part)
        which = far if piece in far[way] else near
        slot = takes_over[step, which] + which[way].index(piece)
        return pltpu.make_async_remote_copy(
            src_ref=sums.at[4 * way + step, at],
            dst_ref=came.at[4 * way + step, at],
            send_sem=rs_send,
            recv_sem=recv.at[way, slot],
            device_id=towards[way],
            device_id_type=MESH,
        )

    def send_sum(step, which, i):
        for way in (UP, DOWN):
            piece = which[way][i]
            at = pl.ds(piece * part, part)
            value = acc[4 + step if way == UP else 4 - step, at]
            if step > 1 or (step == 1 and which is far):
                reduce(way, step - 1, piece).wait_recv()
                value = value + came[4 * way + step - 1, at].astype(F32)
            sums[4 * way + step, at] = value.astype(BF16)
            reduce(way, step, piece).start()

    pass_on(0, far, 0)
    pass_on(0, far, 1)
    pltpu.make_async_copy(own, own, w_load).wait()
    for i in range(3):
        from_partner(i).start()
    pass_on(0, near, 0)
    pass_on(0, near, 1)
    pass_on(1, far, 0)
    pass_on(1, far, 1)
    pass_on(1, near, 0)
    pass_on(2, far, 0)
    arrived_weights(0)
    pass_on(2, far, 1)
    pass_on(1, near, 1)
    arrived_weights(1)
    pass_on(3, far, 0)
    arrived_weights(2)
    pass_on(3, far, 1)
    pass_on(2, near, 0)
    for i in range(3):
        hand_on(i).wait_recv()
    work((3, half, half), (5, 0, half))
    pass_on(2, near, 1)
    work((1, 0, rows), (7, 0, rows))
    send_sum(1, near, 0)
    for way in (UP, DOWN):
        for piece in far[way]:
            gather(way, 3, piece).wait_recv()
    work((4, 0, rows))
    send_sum(0, far, 1)
    send_sum(0, far, 0)
    work((2, 0, rows), (6, 0, rows))
    send_sum(1, near, 1)
    for way in (UP, DOWN):
        for piece in near[way]:
            gather(way, 2, piece).wait_recv()
    work((3, 0, half), (5, half, half))
    send_sum(2, near, 0)
    send_sum(1, far, 1)
    send_sum(1, far, 0)
    work((0, 0, rows))
    send_sum(2, near, 1)
    send_sum(2, far, 1)
    send_sum(2, far, 0)
    send_sum(3, near, 1)
    send_sum(3, near, 0)
    send_sum(3, far, 1)
    send_sum(3, far, 0)
    for which in (near, far):
        for i in (0, 1):
            for way in (UP, DOWN):
                piece = which[way][i]
                at = pl.ds(piece * part, part)
                reduce(way, 3, piece).wait_recv()
                value = acc[0, at] + came[4 * way + 3, at].astype(F32)
                if which is near:
                    acc[0, at] = value
                else:
                    out_ref[at] = value.astype(BF16)

    for sent, sem in ((x.at[pl.ds(0, 7)], ag_send), (sums.at[pl.ds(0, 7)], rs_send), (own, w_send)):
        pltpu.make_async_copy(sent, sent, sem).wait()


def shards(tokens, smooth_scale, gate_weight, up_weight, down_weight):
    rows, width = tokens.shape
    units = gate_weight.shape[0]
    here = pl.BlockSpec(memory_space=pltpu.HBM)
    operands = (tokens, smooth_scale, gate_weight, up_weight, down_weight)
    dma = pltpu.SemaphoreType.DMA
    return pl.pallas_call(
        kernel,
        out_shape=pltpu.VMEM((rows, width), BF16),
        in_specs=[here] * 5,
        out_specs=pl.BlockSpec(memory_space=pltpu.VMEM),
        scratch_shapes=[
            pltpu.VMEM((rows, width), BF16),
            pltpu.VMEM((width,), F32),
            pltpu.VMEM((8, rows, width), BF16),
            pltpu.VMEM((3, 2 * units, width), BF16),
            pltpu.VMEM((8, rows, width), F32),
            pltpu.VMEM((8, rows, width), BF16),
            pltpu.VMEM((8, rows, width), BF16),
            dma((2,)),
            dma,
            dma,
            dma((2, 14)),
            dma,
            dma,
            dma((3,)),
            dma((3,)),
        ],
        compiler_params=pltpu.CompilerParams(
            collective_id=0, has_side_effects=True, vmem_limit_bytes=48 << 20
        ),
    )(*(pltpu.with_memory_space_constraint(o, pltpu.HBM) for o in operands))


def solution(mesh):
    return jax.shard_map(
        shards,
        mesh=mesh,
        in_specs=(
            P(("dp", "tensor"), None),
            P(),
            P("tensor", None),
            P("tensor", None),
            P("tensor", None),
        ),
        out_specs=P(("dp", "tensor"), None),
        check_vma=False,
    )
```

```python
import jax
import jax.numpy as jnp
from jax import lax
from jax.experimental import pallas as pl
from jax.experimental.pallas import tpu as pltpu
from jax.sharding import PartitionSpec as P

MESH = pl.DeviceIdType.MESH
BF16, F32 = jnp.bfloat16, jnp.float32
ROWS_BY_COLS = (((1,), (1,)), ((), ()))
UP, DOWN = 0, 1
FAR_PIECES, NEAR_PIECES = 2, 2


def kernel(
    tokens_ref, scale_ref, gate_ref, up_ref, down_ref, out_ref,
    raw, scale, x, w, acc, sums, came,
    load_sem, ag_send, rs_send, recv, w_load, w_send, w_recv, f_recv,
):
    dp, t = lax.axis_index("dp"), lax.axis_index("tensor")
    core, x_hi, x_lo = dp & 1, (dp >> 1) & 1, t & 1
    other_t = t + 1 - 2 * x_lo
    sibling = (dp + 1 - 2 * core, t)
    partner = (dp + core * (2 - 4 * x_hi), other_t)
    barrier = pltpu.get_barrier_semaphore()
    for device in (partner, (dp, (t + 2) & 15), (dp, (t + 14) & 15), sibling):
        pl.semaphore_signal(barrier, inc=1, device_id=device, device_id_type=MESH)

    rows = tokens_ref.shape[0]
    half = rows // 2
    units = gate_ref.shape[0]
    big = (units // 2 + 15) // 16 * 16
    small = units - big

    own = w.at[:, pl.ds(0, units)]
    loads = [
        pltpu.make_async_copy(tokens_ref, raw, load_sem.at[0]),
        pltpu.make_async_copy(scale_ref, scale, load_sem.at[1]),
    ]
    for load in loads:
        load.start()

    for load in loads:
        load.wait()
    for i, ref in enumerate((gate_ref, up_ref, down_ref)):
        pltpu.make_async_copy(ref, w.at[i, pl.ds(0, units)], w_load).start()
    inverse = 1.0 / scale[...][None, :]
    x[0] = (raw[...].astype(F32) * inverse).astype(BF16)
    pl.semaphore_wait(barrier, 4)

    ways = (UP, DOWN)
    far, near = 0, 1

    pieces = (FAR_PIECES, NEAR_PIECES)

    def piece_at(way, which, i):
        size = half // pieces[which]
        return pl.ds(pl.multiple_of(i * size + half * (way if which == near else 1 - way), size), size)

    def towards(way):
        return (dp, (t + 2 + 12 * way) & 15)

    def gather(way, hop, which, i):
        here = hop + way * (8 - 2 * hop) if hop else 0
        there = hop + 1 + way * (6 - 2 * hop)
        at = piece_at(way, which, i)
        return pltpu.make_async_remote_copy(
            src_ref=x.at[here, at],
            dst_ref=x.at[there, at],
            send_sem=ag_send,
            recv_sem=recv.at[way, sum(pieces) * hop + which * FAR_PIECES + i],
            device_id=towards(way),
            device_id_type=MESH,
        )

    def pass_on(hop, which, i):
        for way in ways:
            if hop:
                gather(way, hop - 1, which, i).wait_recv()
            gather(way, hop, which, i).start()

    def from_partner(i):
        which, start, size = ((core, 0, big), (core, big, small), (2, core * small, big))[i]
        return pltpu.make_async_remote_copy(
            src_ref=w.at[which, pl.ds(pl.multiple_of(start, 16), size)],
            dst_ref=w.at[which, pl.ds(pl.multiple_of(start + units, 16), size)],
            send_sem=w_send,
            recv_sem=w_recv.at[i],
            device_id=partner,
            device_id_type=MESH,
        )

    def hand_on(i):
        which, start, size = ((core, 0, big), (core, big, small), (2, core * big, small))[i]
        at = pl.ds(pl.multiple_of(start + units, 16), size)
        return pltpu.make_async_remote_copy(
            src_ref=w.at[which, at],
            dst_ref=w.at[which, at],
            send_sem=w_send,
            recv_sem=f_recv.at[i],
            device_id=sibling,
            device_id_type=MESH,
        )

    def arrived_weights(i):
        from_partner(i).wait_recv()
        hand_on(i).start()

    def work(*blocks):
        tile = jnp.concatenate([x[s, a : a + n] for s, a, n in blocks], axis=0)
        gate = lax.dot_general(tile, w[0], ROWS_BY_COLS, preferred_element_type=F32)
        up = lax.dot_general(tile, w[1], ROWS_BY_COLS, preferred_element_type=F32)
        hidden = (gate / (1.0 + jnp.exp(-gate)) * up).astype(BF16)
        result = jnp.dot(hidden, w[2], preferred_element_type=F32)
        row = 0
        for s, a, n in blocks:
            acc[s, a : a + n] = result[row : row + n]
            row += n

    def slots(hop, which):
        start = sum(pieces) * hop + which * FAR_PIECES
        return list(range(start, start + pieces[which]))

    takes_over = {
        (0, far): slots(1, far),
        (1, near): slots(0, far)[:NEAR_PIECES],
        (1, far): slots(0, far)[NEAR_PIECES:] + slots(0, near),
        (2, near): slots(2, far)[:NEAR_PIECES],
        (2, far): slots(2, far)[NEAR_PIECES:] + slots(1, near),
        (3, near): slots(2, near),
        (3, far): slots(3, far),
    }

    def reduce(way, step, which, i):
        at = piece_at(way, which, i)
        return pltpu.make_async_remote_copy(
            src_ref=sums.at[4 * way + step, at],
            dst_ref=came.at[4 * way + step, at],
            send_sem=rs_send,
            recv_sem=recv.at[way, takes_over[step, which][i]],
            device_id=towards(way),
            device_id_type=MESH,
        )

    def send_sum(step, which, i):
        for way in ways:
            at = piece_at(way, which, i)
            value = acc[4 + step - 2 * step * way, at]
            if step > 1 or (step == 1 and which == far):
                reduce(way, step - 1, which, i).wait_recv()
                value = value + came[4 * way + step - 1, at].astype(F32)
            sums[4 * way + step, at] = value.astype(BF16)
            reduce(way, step, which, i).start()

    pass_on(0, far, 0)
    pass_on(0, far, 1)
    pltpu.make_async_copy(own, own, w_load).wait()
    for i in range(3):
        from_partner(i).start()
    pass_on(0, near, 0)
    pass_on(0, near, 1)
    pass_on(1, far, 0)
    pass_on(1, far, 1)
    pass_on(1, near, 0)
    pass_on(2, far, 0)
    arrived_weights(0)
    pass_on(2, far, 1)
    pass_on(1, near, 1)
    arrived_weights(1)
    pass_on(3, far, 0)
    arrived_weights(2)
    pass_on(3, far, 1)
    pass_on(2, near, 0)
    for i in range(3):
        hand_on(i).wait_recv()
    work((3, half, half), (5, 0, half))
    pass_on(2, near, 1)
    work((1, 0, rows), (7, 0, rows))
    send_sum(1, near, 0)
    for i in range(FAR_PIECES):
        for way in ways:
            gather(way, 3, far, i).wait_recv()
    work((4, 0, rows))
    send_sum(0, far, 1)
    send_sum(0, far, 0)
    work((2, 0, rows), (6, 0, rows))
    send_sum(1, near, 1)
    for i in range(NEAR_PIECES):
        for way in ways:
            gather(way, 2, near, i).wait_recv()
    work((3, 0, half), (5, half, half))
    send_sum(2, near, 0)
    send_sum(1, far, 1)
    send_sum(1, far, 0)
    work((0, 0, rows))
    send_sum(2, near, 1)
    send_sum(2, far, 1)
    send_sum(2, far, 0)
    send_sum(3, near, 0)
    send_sum(3, near, 1)
    send_sum(3, far, 1)
    send_sum(3, far, 0)
    for which in (near, far):
        for i in range(pieces[which]):
            for way in ways:
                at = piece_at(way, which, i)
                reduce(way, 3, which, i).wait_recv()
                value = acc[0, at] + came[4 * way + 3, at].astype(F32)
                if which == near:
                    acc[0, at] = value
                else:
                    out_ref[at] = value.astype(BF16)

    for sent, sem in ((x.at[pl.ds(0, 7)], ag_send), (sums.at[pl.ds(0, 7)], rs_send), (own, w_send)):
        pltpu.make_async_copy(sent, sent, sem).wait()


def shards(tokens, smooth_scale, gate_weight, up_weight, down_weight):
    rows, width = tokens.shape
    units = gate_weight.shape[0]
    here = pl.BlockSpec(memory_space=pltpu.HBM)
    operands = (tokens, smooth_scale, gate_weight, up_weight, down_weight)
    dma = pltpu.SemaphoreType.DMA
    return pl.pallas_call(
        kernel,
        out_shape=pltpu.VMEM((rows, width), BF16),
        in_specs=[here] * 5,
        out_specs=pl.BlockSpec(memory_space=pltpu.VMEM),
        scratch_shapes=[
            pltpu.VMEM((rows, width), BF16),
            pltpu.VMEM((width,), F32),
            pltpu.VMEM((8, rows, width), BF16),
            pltpu.VMEM((3, 2 * units, width), BF16),
            pltpu.VMEM((8, rows, width), F32),
            pltpu.VMEM((8, rows, width), BF16),
            pltpu.VMEM((8, rows, width), BF16),
            dma((2,)),
            dma,
            dma,
            dma((2, 4 * FAR_PIECES + 3 * NEAR_PIECES)),
            dma,
            dma,
            dma((3,)),
            dma((3,)),
        ],
        compiler_params=pltpu.CompilerParams(
            collective_id=0, has_side_effects=True, vmem_limit_bytes=48 << 20
        ),
    )(*(pltpu.with_memory_space_constraint(o, pltpu.HBM) for o in operands))


def solution(mesh):
    return jax.shard_map(
        shards,
        mesh=mesh,
        in_specs=(
            P(("dp", "tensor"), None),
            P(),
            P("tensor", None),
            P("tensor", None),
            P("tensor", None),
        ),
        out_specs=P(("dp", "tensor"), None),
        check_vma=False,
    )
```

```python
import jax
import jax.numpy as jnp
from jax import lax
from jax.experimental import pallas as pl
from jax.experimental.pallas import tpu as pltpu
from jax.sharding import PartitionSpec as P

MESH = pl.DeviceIdType.MESH
BF16, F32 = jnp.bfloat16, jnp.float32
ROWS_BY_COLS = (((1,), (1,)), ((), ()))
UP, DOWN = 0, 1
FAR_PIECES, NEAR_PIECES = 2, 2


def kernel(
    tokens_ref, scale_ref, gate_ref, up_ref, down_ref, out_ref,
    raw, scale, x, w, acc, sums, came,
    load_sem, ag_send, rs_send, recv, w_load, w_send, w_recv, f_recv,
):
    dp, t = lax.axis_index("dp"), lax.axis_index("tensor")
    core, x_hi, x_lo = dp & 1, (dp >> 1) & 1, t & 1
    other_t = t + 1 - 2 * x_lo
    sibling = (dp + 1 - 2 * core, t)
    partner = (dp + core * (2 - 4 * x_hi), other_t)
    barrier = pltpu.get_barrier_semaphore()
    for device in (partner, (dp, (t + 2) & 15), (dp, (t + 14) & 15), sibling):
        pl.semaphore_signal(barrier, inc=1, device_id=device, device_id_type=MESH)

    rows = tokens_ref.shape[0]
    half = rows // 2
    units = gate_ref.shape[0]
    big = (units // 2 + 15) // 16 * 16
    small = units - big

    own = w.at[:, pl.ds(0, units)]
    loads = [
        pltpu.make_async_copy(tokens_ref, raw, load_sem.at[0]),
        pltpu.make_async_copy(scale_ref, scale, load_sem.at[1]),
    ]
    for load in loads:
        load.start()

    for load in loads:
        load.wait()
    for i, ref in enumerate((gate_ref, up_ref, down_ref)):
        pltpu.make_async_copy(ref, w.at[i, pl.ds(0, units)], w_load).start()
    inverse = 1.0 / scale[...][None, :]
    x[0] = (raw[...].astype(F32) * inverse).astype(BF16)
    pl.semaphore_wait(barrier, 4)

    ways = (UP, DOWN)
    far, near = 0, 1

    pieces = (FAR_PIECES, NEAR_PIECES)

    def piece_at(way, which, i):
        size = half // pieces[which]
        return pl.ds(pl.multiple_of(i * size + half * (way if which == near else 1 - way), size), size)

    def towards(way):
        return (dp, (t + 2 + 12 * way) & 15)

    def gather(way, hop, which, i):
        here = hop + way * (8 - 2 * hop) if hop else 0
        there = hop + 1 + way * (6 - 2 * hop)
        at = piece_at(way, which, i)
        return pltpu.make_async_remote_copy(
            src_ref=x.at[here, at],
            dst_ref=x.at[there, at],
            send_sem=ag_send,
            recv_sem=recv.at[way, sum(pieces) * hop + which * FAR_PIECES + i],
            device_id=towards(way),
            device_id_type=MESH,
        )

    def pass_on(hop, which, i):
        for way in ways:
            if hop:
                gather(way, hop - 1, which, i).wait_recv()
            gather(way, hop, which, i).start()

    def from_partner(i):
        which, start, size = ((core, 0, big), (core, big, small), (2, core * small, big))[i]
        return pltpu.make_async_remote_copy(
            src_ref=w.at[which, pl.ds(pl.multiple_of(start, 16), size)],
            dst_ref=w.at[which, pl.ds(pl.multiple_of(start + units, 16), size)],
            send_sem=w_send,
            recv_sem=w_recv.at[i],
            device_id=partner,
            device_id_type=MESH,
        )

    def hand_on(i):
        which, start, size = ((core, 0, big), (core, big, small), (2, core * big, small))[i]
        at = pl.ds(pl.multiple_of(start + units, 16), size)
        return pltpu.make_async_remote_copy(
            src_ref=w.at[which, at],
            dst_ref=w.at[which, at],
            send_sem=w_send,
            recv_sem=f_recv.at[i],
            device_id=sibling,
            device_id_type=MESH,
        )

    def arrived_weights(i):
        from_partner(i).wait_recv()
        hand_on(i).start()

    def work(*blocks):
        tile = jnp.concatenate([x[s, a : a + n] for s, a, n in blocks], axis=0)
        gate = lax.dot_general(tile, w[0], ROWS_BY_COLS, preferred_element_type=F32)
        up = lax.dot_general(tile, w[1], ROWS_BY_COLS, preferred_element_type=F32)
        hidden = (gate / (1.0 + jnp.exp(-gate)) * up).astype(BF16)
        result = jnp.dot(hidden, w[2], preferred_element_type=F32)
        row = 0
        for s, a, n in blocks:
            acc[s, a : a + n] = result[row : row + n]
            row += n

    def slots(hop, which):
        start = sum(pieces) * hop + which * FAR_PIECES
        return list(range(start, start + pieces[which]))

    takes_over = {
        (0, far): slots(1, far),
        (1, near): slots(0, far)[:NEAR_PIECES],
        (1, far): slots(0, far)[NEAR_PIECES:] + slots(0, near),
        (2, near): slots(2, far)[:NEAR_PIECES],
        (2, far): slots(2, far)[NEAR_PIECES:] + slots(1, near),
        (3, near): slots(2, near),
        (3, far): slots(3, far),
    }

    def reduce(way, step, which, i):
        at = piece_at(way, which, i)
        return pltpu.make_async_remote_copy(
            src_ref=sums.at[4 * way + step, at],
            dst_ref=came.at[4 * way + step, at],
            send_sem=rs_send,
            recv_sem=recv.at[way, takes_over[step, which][i]],
            device_id=towards(way),
            device_id_type=MESH,
        )

    def send_sum(step, which, i):
        for way in ways:
            at = piece_at(way, which, i)
            value = acc[4 + step - 2 * step * way, at]
            if step > 1 or (step == 1 and which == far):
                reduce(way, step - 1, which, i).wait_recv()
                value = value + came[4 * way + step - 1, at].astype(F32)
            sums[4 * way + step, at] = value.astype(BF16)
            reduce(way, step, which, i).start()

    pass_on(0, far, 0)
    pass_on(0, far, 1)
    pltpu.make_async_copy(own, own, w_load).wait()
    for i in range(3):
        from_partner(i).start()
    pass_on(0, near, 0)
    pass_on(0, near, 1)
    pass_on(1, far, 0)
    pass_on(1, far, 1)
    pass_on(1, near, 0)
    pass_on(2, far, 0)
    arrived_weights(0)
    pass_on(2, far, 1)
    pass_on(1, near, 1)
    arrived_weights(1)
    pass_on(3, far, 0)
    arrived_weights(2)
    pass_on(3, far, 1)
    pass_on(2, near, 0)
    for i in range(3):
        hand_on(i).wait_recv()
    work((3, half, half), (5, 0, half))
    pass_on(2, near, 1)
    work((1, 0, rows), (7, 0, rows))
    send_sum(1, near, 0)
    for i in range(FAR_PIECES):
        for way in ways:
            gather(way, 3, far, i).wait_recv()
    work((4, 0, rows))
    send_sum(0, far, 1)
    send_sum(0, far, 0)
    work((2, 0, rows), (6, 0, rows))
    send_sum(1, near, 1)
    for i in range(NEAR_PIECES):
        for way in ways:
            gather(way, 2, near, i).wait_recv()
    work((3, 0, half), (5, half, half))
    send_sum(2, near, 0)
    send_sum(1, far, 1)
    send_sum(1, far, 0)
    send_sum(2, near, 1)
    send_sum(2, far, 1)
    send_sum(2, far, 0)
    send_sum(3, near, 0)
    send_sum(3, near, 1)
    send_sum(3, far, 1)
    send_sum(3, far, 0)
    work((0, 0, rows))
    for which in (near, far):
        for i in range(pieces[which]):
            for way in ways:
                at = piece_at(way, which, i)
                reduce(way, 3, which, i).wait_recv()
                value = acc[0, at] + came[4 * way + 3, at].astype(F32)
                if which == near:
                    acc[0, at] = value
                else:
                    out_ref[at] = value.astype(BF16)

    for sent, sem in ((x.at[pl.ds(0, 7)], ag_send), (sums.at[pl.ds(0, 7)], rs_send), (own, w_send)):
        pltpu.make_async_copy(sent, sent, sem).wait()


def shards(tokens, smooth_scale, gate_weight, up_weight, down_weight):
    rows, width = tokens.shape
    units = gate_weight.shape[0]
    here = pl.BlockSpec(memory_space=pltpu.HBM)
    operands = (tokens, smooth_scale, gate_weight, up_weight, down_weight)
    dma = pltpu.SemaphoreType.DMA
    return pl.pallas_call(
        kernel,
        out_shape=pltpu.VMEM((rows, width), BF16),
        in_specs=[here] * 5,
        out_specs=pl.BlockSpec(memory_space=pltpu.VMEM),
        scratch_shapes=[
            pltpu.VMEM((rows, width), BF16),
            pltpu.VMEM((width,), F32),
            pltpu.VMEM((8, rows, width), BF16),
            pltpu.VMEM((3, 2 * units, width), BF16),
            pltpu.VMEM((8, rows, width), F32),
            pltpu.VMEM((8, rows, width), BF16),
            pltpu.VMEM((8, rows, width), BF16),
            dma((2,)),
            dma,
            dma,
            dma((2, 4 * FAR_PIECES + 3 * NEAR_PIECES)),
            dma,
            dma,
            dma((3,)),
            dma((3,)),
        ],
        compiler_params=pltpu.CompilerParams(
            collective_id=0, has_side_effects=True, vmem_limit_bytes=48 << 20
        ),
    )(*(pltpu.with_memory_space_constraint(o, pltpu.HBM) for o in operands))


def solution(mesh):
    return jax.shard_map(
        shards,
        mesh=mesh,
        in_specs=(
            P(("dp", "tensor"), None),
            P(),
            P("tensor", None),
            P("tensor", None),
            P("tensor", None),
        ),
        out_specs=P(("dp", "tensor"), None),
        check_vma=False,
    )
```

```python
import jax
import jax.numpy as jnp
from jax import lax
from jax.experimental import pallas as pl
from jax.experimental.pallas import tpu as pltpu
from jax.sharding import PartitionSpec as P

MESH = pl.DeviceIdType.MESH
BF16, F32 = jnp.bfloat16, jnp.float32
ROWS_BY_COLS = (((1,), (1,)), ((), ()))
UP, DOWN = 0, 1
FAR_PIECES, NEAR_PIECES = 2, 2


def kernel(
    tokens_ref, scale_ref, gate_ref, up_ref, down_ref, out_ref,
    raw, scale, x, w, acc, sums, came,
    load_sem, ag_send, rs_send, recv, w_load, w_send, w_recv, f_recv,
):
    dp, t = lax.axis_index("dp"), lax.axis_index("tensor")
    core, x_hi, x_lo = dp & 1, (dp >> 1) & 1, t & 1
    other_t = t + 1 - 2 * x_lo
    sibling = (dp + 1 - 2 * core, t)
    partner = (dp + core * (2 - 4 * x_hi), other_t)
    barrier = pltpu.get_barrier_semaphore()
    for device in (partner, (dp, (t + 2) & 15), (dp, (t + 14) & 15), sibling):
        pl.semaphore_signal(barrier, inc=1, device_id=device, device_id_type=MESH)

    rows = tokens_ref.shape[0]
    half = rows // 2
    units = gate_ref.shape[0]
    big = (units // 2 + 15) // 16 * 16
    small = units - big

    own = w.at[:, pl.ds(0, units)]
    loads = [
        pltpu.make_async_copy(tokens_ref, raw, load_sem.at[0]),
        pltpu.make_async_copy(scale_ref, scale, load_sem.at[1]),
    ]
    for load in loads:
        load.start()

    for load in loads:
        load.wait()
    for i, ref in enumerate((gate_ref, up_ref, down_ref)):
        pltpu.make_async_copy(ref, w.at[i, pl.ds(0, units)], w_load).start()
    inverse = 1.0 / scale[...][None, :]
    x[0] = (raw[...].astype(F32) * inverse).astype(BF16)
    pl.semaphore_wait(barrier, 4)

    ways = (UP, DOWN)
    far, near = 0, 1

    pieces = (FAR_PIECES, NEAR_PIECES)

    def piece_at(way, which, i):
        size = half // pieces[which]
        return pl.ds(pl.multiple_of(i * size + half * (way if which == near else 1 - way), size), size)

    def towards(way):
        return (dp, (t + 2 + 12 * way) & 15)

    def gather(way, hop, which, i):
        here = hop + way * (8 - 2 * hop) if hop else 0
        there = hop + 1 + way * (6 - 2 * hop)
        at = piece_at(way, which, i)
        return pltpu.make_async_remote_copy(
            src_ref=x.at[here, at],
            dst_ref=x.at[there, at],
            send_sem=ag_send,
            recv_sem=recv.at[way, sum(pieces) * hop + which * FAR_PIECES + i],
            device_id=towards(way),
            device_id_type=MESH,
        )

    def pass_on(hop, which, i):
        for way in ways:
            if hop:
                gather(way, hop - 1, which, i).wait_recv()
            gather(way, hop, which, i).start()

    def from_partner(i):
        which, start, size = ((core, 0, big), (core, big, small), (2, core * small, big))[i]
        return pltpu.make_async_remote_copy(
            src_ref=w.at[which, pl.ds(pl.multiple_of(start, 16), size)],
            dst_ref=w.at[which, pl.ds(pl.multiple_of(start + units, 16), size)],
            send_sem=w_send,
            recv_sem=w_recv.at[i],
            device_id=partner,
            device_id_type=MESH,
        )

    def hand_on(i):
        which, start, size = ((core, 0, big), (core, big, small), (2, core * big, small))[i]
        at = pl.ds(pl.multiple_of(start + units, 16), size)
        return pltpu.make_async_remote_copy(
            src_ref=w.at[which, at],
            dst_ref=w.at[which, at],
            send_sem=w_send,
            recv_sem=f_recv.at[i],
            device_id=sibling,
            device_id_type=MESH,
        )

    def arrived_weights(i):
        from_partner(i).wait_recv()
        hand_on(i).start()

    def work(*blocks):
        tile = jnp.concatenate([x[s, a : a + n] for s, a, n in blocks], axis=0)
        gate = lax.dot_general(tile, w[0], ROWS_BY_COLS, preferred_element_type=F32)
        up = lax.dot_general(tile, w[1], ROWS_BY_COLS, preferred_element_type=F32)
        hidden = (gate / (1.0 + jnp.exp(-gate)) * up).astype(BF16)
        result = jnp.dot(hidden, w[2], preferred_element_type=F32)
        row = 0
        for s, a, n in blocks:
            acc[s, a : a + n] = result[row : row + n]
            row += n

    def slots(hop, which):
        start = sum(pieces) * hop + which * FAR_PIECES
        return list(range(start, start + pieces[which]))

    takes_over = {
        (0, far): slots(1, far),
        (1, near): slots(0, far)[:NEAR_PIECES],
        (1, far): slots(0, far)[NEAR_PIECES:] + slots(0, near),
        (2, near): slots(2, far)[:NEAR_PIECES],
        (2, far): slots(2, far)[NEAR_PIECES:] + slots(1, near),
        (3, near): slots(2, near),
        (3, far): slots(3, far),
    }

    def reduce(way, step, which, i):
        at = piece_at(way, which, i)
        return pltpu.make_async_remote_copy(
            src_ref=sums.at[4 * way + step, at],
            dst_ref=came.at[4 * way + step, at],
            send_sem=rs_send,
            recv_sem=recv.at[way, takes_over[step, which][i]],
            device_id=towards(way),
            device_id_type=MESH,
        )

    def send_sum(step, which, i):
        for way in ways:
            at = piece_at(way, which, i)
            value = acc[4 + step - 2 * step * way, at]
            if step > 1 or (step == 1 and which == far):
                reduce(way, step - 1, which, i).wait_recv()
                value = value + came[4 * way + step - 1, at].astype(F32)
            sums[4 * way + step, at] = value.astype(BF16)
            reduce(way, step, which, i).start()

    pass_on(0, far, 0)
    pass_on(0, far, 1)
    pass_on(0, near, 0)
    pass_on(0, near, 1)
    pltpu.make_async_copy(own, own, w_load).wait()
    for i in range(3):
        from_partner(i).start()
    pass_on(1, far, 0)
    pass_on(1, far, 1)
    pass_on(1, near, 0)
    pass_on(2, far, 0)
    arrived_weights(0)
    pass_on(2, far, 1)
    pass_on(1, near, 1)
    arrived_weights(1)
    pass_on(3, far, 0)
    arrived_weights(2)
    pass_on(3, far, 1)
    pass_on(2, near, 0)
    for i in range(3):
        hand_on(i).wait_recv()
    work((3, half, half), (5, 0, half))
    pass_on(2, near, 1)
    work((1, 0, rows), (7, 0, rows))
    send_sum(1, near, 0)
    for i in range(FAR_PIECES):
        for way in ways:
            gather(way, 3, far, i).wait_recv()
    work((4, 0, rows))
    send_sum(0, far, 1)
    send_sum(0, far, 0)
    work((2, 0, rows), (6, 0, rows))
    send_sum(1, near, 1)
    for i in range(NEAR_PIECES):
        for way in ways:
            gather(way, 2, near, i).wait_recv()
    work((3, 0, half), (5, half, half))
    send_sum(2, near, 0)
    send_sum(1, far, 1)
    send_sum(1, far, 0)
    send_sum(2, near, 1)
    send_sum(2, far, 1)
    send_sum(2, far, 0)
    send_sum(3, near, 0)
    send_sum(3, near, 1)
    send_sum(3, far, 1)
    send_sum(3, far, 0)
    work((0, 0, rows))
    for which in (near, far):
        for i in range(pieces[which]):
            for way in ways:
                at = piece_at(way, which, i)
                reduce(way, 3, which, i).wait_recv()
                value = acc[0, at] + came[4 * way + 3, at].astype(F32)
                if which == near:
                    acc[0, at] = value
                else:
                    out_ref[at] = value.astype(BF16)

    for sent, sem in ((x.at[pl.ds(0, 7)], ag_send), (sums.at[pl.ds(0, 7)], rs_send), (own, w_send)):
        pltpu.make_async_copy(sent, sent, sem).wait()


def shards(tokens, smooth_scale, gate_weight, up_weight, down_weight):
    rows, width = tokens.shape
    units = gate_weight.shape[0]
    here = pl.BlockSpec(memory_space=pltpu.HBM)
    operands = (tokens, smooth_scale, gate_weight, up_weight, down_weight)
    dma = pltpu.SemaphoreType.DMA
    return pl.pallas_call(
        kernel,
        out_shape=pltpu.VMEM((rows, width), BF16),
        in_specs=[here] * 5,
        out_specs=pl.BlockSpec(memory_space=pltpu.VMEM),
        scratch_shapes=[
            pltpu.VMEM((rows, width), BF16),
            pltpu.VMEM((width,), F32),
            pltpu.VMEM((8, rows, width), BF16),
            pltpu.VMEM((3, 2 * units, width), BF16),
            pltpu.VMEM((8, rows, width), F32),
            pltpu.VMEM((8, rows, width), BF16),
            pltpu.VMEM((8, rows, width), BF16),
            dma((2,)),
            dma,
            dma,
            dma((2, 4 * FAR_PIECES + 3 * NEAR_PIECES)),
            dma,
            dma,
            dma((3,)),
            dma((3,)),
        ],
        compiler_params=pltpu.CompilerParams(
            collective_id=0, has_side_effects=True, vmem_limit_bytes=48 << 20
        ),
    )(*(pltpu.with_memory_space_constraint(o, pltpu.HBM) for o in operands))


def solution(mesh):
    return jax.shard_map(
        shards,
        mesh=mesh,
        in_specs=(
            P(("dp", "tensor"), None),
            P(),
            P("tensor", None),
            P("tensor", None),
            P("tensor", None),
        ),
        out_specs=P(("dp", "tensor"), None),
        check_vma=False,
    )
```
